32 devices in a mesh: tm: 8 (over z, x), space: 4 (over y, core).
Axes of the slice: x: 2, y: 2, z: 4, core: 2. Of those that a mesh axis runs over, the one named last changes fastest.
Arguments:
- query_states: bfloat16 [8, 1024, 2560], P('tm', 'space'), may hold values from -45 to 45
- key_states: bfloat16 [8, 1024, 2560], P('tm', 'space'), may hold values from -4 to 4
- value_states: bfloat16 [8, 1024, 2560], P('tm', 'space'), may hold values from -6 to 6
- history: int32 [8], P('tm'), may hold values from 0 to 2, as said below
- neighbours: int32 [8, 4, 2], P('tm', 'space'), may hold values 0 or 1
Outputs:
- attended: bfloat16 [8, 1024, 2560], P('tm', 'space')
The draws below stay inside these ranges and needn't reach their ends.
Inputs may be any that keep to these rules, and one draw needn't show every extreme that they name: Some segment has history exactly 2 in every draw.
All inputs are finite; a program needn't handle non-finite values. No bound on the sum of `neighbours` on one device may be relied on, other than what follows from the above.
Results may differ from the reference program's by a relative error of at most 0.005.
Values may be sent and summed in bfloat16 or wider, within the bound.
A program may use at most 128 MiB of HBM per device.

```python
import jax
import jax.numpy as jnp
from jax import lax

HEADS = 20
HEAD_DIM = 128
FR = 1
TILE = 256
HIST_MAX = 2
NBLOCKS = 8
NF = 8
NTOK = 1024
N_TM = 8
N_SPACE = 4


def draw_pair(key):
    shape = (NF, NTOK, HEADS * HEAD_DIM)
    key_vals = jnp.clip(jax.random.normal(jax.random.fold_in(key, 11), shape, jnp.float32), -4.0, 4.0)
    query_vals = 3.0 * jnp.clip(jax.random.normal(jax.random.fold_in(key, 12), shape, jnp.float32), -4.0, 4.0)
    return (query_vals, key_vals)


def draw_query_states(key, part):
    return draw_pair(key)[0].astype(jnp.bfloat16)


def draw_key_states(key, part):
    return draw_pair(key)[1].astype(jnp.bfloat16)


def draw_history(key, part):
    lengths = jax.random.randint(jax.random.fold_in(key, 21), (NBLOCKS,), 0, HIST_MAX + 1)
    target = jax.random.randint(jax.random.fold_in(key, 22), (), 0, NBLOCKS)
    return jnp.where(jnp.arange(NBLOCKS) == target, HIST_MAX, lengths).astype(jnp.int32)


def with_ends(values, rng, smallest, top_value):
    shape = values.shape
    spot = [jax.random.randint(jax.random.fold_in(rng, axis), (), 0, shape[axis]) for axis in range(len(shape))]
    values = values.at[tuple(spot)].set(smallest)
    longest = shape.index(max(shape))
    spot[longest] = (spot[longest] + 1) % shape[longest]
    return values.at[tuple(spot)].set(top_value)


def steps_of(own_key, extent, pieces, low, high):
    gain = 1.0
    for position, blocks in pieces:
        heights = jax.random.uniform(jax.random.fold_in(jax.random.fold_in(own_key, 6), position), (blocks,), jnp.float32, low / len(pieces), high / len(pieces))
        gain = gain * jnp.repeat(jnp.exp(heights), extent[position] // blocks).reshape((-1,) + (1,) * (len(extent) - 1 - position))
    return gain


def bell_draw(stream_key, dims, spread, bound, shards=(), kind=jnp.bfloat16):
    array = jax.random.normal(stream_key, dims, jnp.float32) * spread
    if len(shards) > 0:
        array = steps_of(stream_key, dims, shards, -0.22, 0.18) * array
    return jnp.clip(array, min=-bound, max=bound).astype(kind)


def setup_inputs(seed: int = 0) -> dict:
    key_of = jax.random.split(jax.random.key(seed), 6)
    return {
        "query_states": draw_query_states(jax.random.fold_in(key_of[5], 71), 0),
        "key_states": draw_key_states(jax.random.fold_in(key_of[5], 71), 0),
        "value_states": bell_draw(key_of[2], (NF, NTOK, HEADS * HEAD_DIM), 1.0, 6.0, ((0, 8), (1, 4))),
        "history": draw_history(jax.random.fold_in(key_of[5], 71), 0),
        "neighbours": with_ends((jax.random.randint(key_of[4], (NBLOCKS, N_SPACE, 2), 0, 4) < 3).astype(jnp.int32), jax.random.fold_in(key_of[4], 1), 0, 1),
    }


def reference(query_states, key_states, value_states, history, neighbours):
    width_all = query_states.shape[2]
    head_count = width_all // HEAD_DIM
    inv_root = 1.0 / (HEAD_DIM ** 0.5)
    key_pad = jnp.pad(key_states, ((HIST_MAX, 0), (TILE, TILE), (0, 0)))
    value_pad = jnp.pad(value_states, ((HIST_MAX, 0), (TILE, TILE), (0, 0)))
    span = HIST_MAX + FR

    def one_block(index):
        seg = (index // N_SPACE).astype(jnp.int32)
        tile_pos = (index % N_SPACE).astype(jnp.int32)
        zero = jnp.zeros((), jnp.int32)
        queries = lax.dynamic_slice(query_states, (seg * FR, tile_pos * TILE, zero), (FR, TILE, width_all))
        key_block = lax.dynamic_slice(key_pad, (seg * FR, tile_pos * TILE, zero), (span, 3 * TILE, width_all))
        value_block = lax.dynamic_slice(value_pad, (seg * FR, tile_pos * TILE, zero), (span, 3 * TILE, width_all))
        query_rows = queries.reshape(FR * TILE, head_count, HEAD_DIM).astype(jnp.float32)
        key_rows = key_block.reshape(span * 3 * TILE, head_count, HEAD_DIM).astype(jnp.float32)
        value_rows = value_block.reshape(span * 3 * TILE, head_count, HEAD_DIM).astype(jnp.float32)
        key_frame = seg * FR - HIST_MAX + jnp.repeat(jnp.arange(span, dtype=jnp.int32), 3 * TILE)
        third = jnp.tile(jnp.arange(3 * TILE, dtype=jnp.int32) // TILE, span)
        left_open = (neighbours[seg, tile_pos, 0] == 1) & (tile_pos > 0)
        right_open = (neighbours[seg, tile_pos, 1] == 1) & (tile_pos < N_SPACE - 1)
        side_ok = jnp.where(third == 0, left_open, jnp.where(third == 2, right_open, True))
        query_frame = seg * FR + jnp.repeat(jnp.arange(FR, dtype=jnp.int32), TILE)
        allowed = (key_frame[None, :] <= query_frame[:, None]) & (key_frame[None, :] >= seg * FR - history[seg]) & (key_frame >= 0)[None, :] & side_ok[None, :]
        scores = jnp.einsum("rhd,khd->hrk", query_rows, key_rows) * inv_root
        scores = jnp.where(allowed[None], scores, -1e30)
        best = jnp.max(scores, axis=-1)
        weights = jnp.where(allowed[None], jnp.exp(scores - best[..., None]), 0.0)
        denom = jnp.sum(weights, axis=-1)
        weights_low = lax.optimization_barrier(weights.astype(jnp.bfloat16)).astype(jnp.float32)
        numer = jnp.einsum("hrk,khd->hrd", weights_low, value_rows)
        result = numer / denom[..., None]
        return jnp.transpose(result, (1, 0, 2)).reshape(FR, TILE, width_all).astype(jnp.bfloat16)

    blocks = lax.map(one_block, jnp.arange(N_TM * N_SPACE, dtype=jnp.int32))
    blocks = blocks.reshape(N_TM, N_SPACE, FR, TILE, width_all)
    return jnp.transpose(blocks, (0, 2, 1, 3, 4)).reshape(NF, NTOK, width_all)
```

```python
import functools
import math

import jax
import jax.numpy as jnp
from jax import lax
from jax.experimental import pallas as pl
from jax.experimental.pallas import tpu as pltpu
from jax.sharding import PartitionSpec as P

HEAD_DIM = 128
CHUNK = 256
MATE0, CROSS0, SAME2, SAME1, MATE1, MATE2, CROSS1, CROSS2 = range(8)
BIG = 1e30
LEAD_OWN = 5
LEAD_1 = 2
LEAD_2 = 1


def kernel(ns, nt, hist_ref, side_ref, q_ref, k_ref, v_ref, o_ref, kbuf, vbuf, send_sem, recv_sem):
    rows, width = k_ref.shape
    chunks = width // CHUNK
    s = lax.axis_index("tm")
    t = lax.axis_index("space")
    odd = lax.rem(s, 2) == 1
    even = jnp.logical_not(odd)
    t_odd = lax.rem(t, 2) == 1
    mate = jnp.where(t_odd, t - 1, t + 1)
    cross = jnp.where(t_odd, t + 1, t - 1)
    pair = jnp.where(odd, s - 1, s + 1)
    has_cross = (cross >= 0) & (cross < nt)
    up = s + 2 < ns
    has1 = s >= 1
    has2 = s >= 2

    barrier = pltpu.get_barrier_semaphore()

    def greet(ss, tt):
        pl.semaphore_signal(
            barrier, inc=1, device_id=(ss, tt), device_id_type=pl.DeviceIdType.MESH
        )

    greet(s, mate)
    greet(pair, t)

    @pl.when(has_cross)
    def _():
        greet(s, cross)

    @pl.when(up)
    def _():
        greet(s + 2, t)

    @pl.when(has2)
    def _():
        greet(s - 2, t)

    for missing, slots in (
        (jnp.logical_not(has1), (SAME1, MATE1)),
        (jnp.logical_not(has2), (SAME2, MATE2)),
        (jnp.logical_not(has_cross), (CROSS0,)),
        (jnp.logical_not(has_cross & has1), (CROSS1,)),
        (jnp.logical_not(has_cross & has2), (CROSS2,)),
    ):

        @pl.when(missing)
        def _(slots=slots):
            for slot in slots:
                kbuf[slot] = jnp.zeros((rows, width), kbuf.dtype)
                vbuf[slot] = jnp.zeros((rows, width), vbuf.dtype)

    peers = 2
    for there in (has_cross, up, has2):
        peers = peers + jnp.where(there, 1, 0)
    pl.semaphore_wait(barrier, peers)

    def cols(j):
        return pl.ds(pl.multiple_of(j * CHUNK, CHUNK), CHUNK)

    def copies(kind, j, source, ss, tt):
        where = cols(j)
        out = []
        for index, (own, buf) in enumerate(((k_ref, kbuf), (v_ref, vbuf))):
            src = own.at[:, where] if source is None else buf.at[source, :, where]
            out.append(
                pltpu.make_async_remote_copy(
                    src_ref=src,
                    dst_ref=buf.at[kind, :, where],
                    send_sem=send_sem.at[index, kind, j],
                    recv_sem=recv_sem.at[index, kind, j],
                    device_id=(ss, tt),
                    device_id_type=pl.DeviceIdType.MESH,
                )
            )
        return out

    def send(kind, j, source, ss, tt):
        for copy in copies(kind, j, source, ss, tt):
            copy.start()

    def got(kind, j):
        for copy in copies(kind, j, None, s, mate):
            copy.wait_recv()

    def sent(kind, j):
        for copy in copies(kind, j, None, s, mate):
            copy.wait_send()

    def along(j):
        return lax.rem(j, 3) == 1

    def stage_own(j):
        @pl.when(up)
        def _():
            send(SAME2, j, None, s + 2, t)

        @pl.when(even)
        def _():
            send(SAME1, j, None, pair, t)

        @pl.when(has_cross)
        def _():
            send(CROSS0, j, None, s, cross)

        send(MATE0, j, None, s, mate)

    def stage_1(j):
        @pl.when(has2)
        def _():
            got(SAME2, j)

            @pl.when(odd)
            def _():
                send(SAME1, j, SAME2, pair, t)

            @pl.when(has_cross & jnp.logical_not(along(j)))
            def _():
                send(CROSS2, j, SAME2, s, cross)

            send(MATE2, j, SAME2, s, mate)

        @pl.when(has_cross & along(j))
        def _():
            got(CROSS0, j)

            @pl.when(up)
            def _():
                send(CROSS2, j, CROSS0, s + 2, t)

            @pl.when(even)
            def _():
                send(CROSS1, j, CROSS0, pair, t)

    def stage_2(j):
        @pl.when(has1)
        def _():
            got(SAME1, j)

            @pl.when(has_cross & jnp.logical_not(along(j)))
            def _():
                send(CROSS1, j, SAME1, s, cross)

            send(MATE1, j, SAME1, s, mate)

        @pl.when(has_cross & along(j) & has2 & odd)
        def _():
            got(CROSS2, j)
            send(CROSS1, j, CROSS2, pair, t)

    history = hist_ref[0]
    left = (side_ref[0] == 1) & (t > 0)
    right = (side_ref[1] == 1) & (t < nt - 1)
    mate_ok = (t_odd & left) | (jnp.logical_not(t_odd) & right)
    cross_ok = (t_odd & right) | (jnp.logical_not(t_odd) & left)
    one_ok = (history >= 1) & has1
    two_ok = (history >= 2) & has2
    blocks = (
        (None, None),
        (MATE0, mate_ok),
        (CROSS0, cross_ok),
        (SAME1, one_ok),
        (MATE1, one_ok & mate_ok),
        (CROSS1, one_ok & cross_ok),
        (SAME2, two_ok),
        (MATE2, two_ok & mate_ok),
        (CROSS2, two_ok & cross_ok),
    )
    shifts = [
        None if ok is None else jnp.where(ok, jnp.float32(0.0), jnp.float32(BIG))
        for _, ok in blocks
    ]
    factor = math.log2(math.e) / HEAD_DIM**0.5

    def attend(j):
        for part in range(CHUNK // HEAD_DIM):
            where = pl.ds(pl.multiple_of(j * CHUNK + part * HEAD_DIM, HEAD_DIM), HEAD_DIM)
            q = q_ref[:, where]
            scores = []
            top = None
            for (slot, _), shift in zip(blocks, shifts):
                k = k_ref[:, where] if slot is None else kbuf[slot, :, where]
                score = lax.dot_general(
                    q, k, (((1,), (1,)), ((), ())), preferred_element_type=jnp.float32
                )
                scores.append(score)
                top = score if slot is None else jnp.maximum(top, score - shift)
            best = jnp.max(top, axis=1, keepdims=True) * factor
            total = None
            accum = None
            for (slot, _), shift, score in zip(blocks, shifts, scores):
                v = v_ref[:, where] if slot is None else vbuf[slot, :, where]
                floor = best if slot is None else best + shift
                weights = jnp.exp2(score * factor - floor)
                total = weights if slot is None else total + weights
                term = lax.dot_general(
                    weights.astype(jnp.bfloat16),
                    v,
                    (((1,), (0,)), ((), ())),
                    preferred_element_type=jnp.float32,
                )
                accum = term if slot is None else accum + term
            denom = jnp.sum(total, axis=1, keepdims=True)
            o_ref[:, where] = (accum / denom).astype(o_ref.dtype)

    def stage_3(j):
        got(MATE0, j)

        @pl.when(has_cross & jnp.logical_not(along(j)))
        def _():
            got(CROSS0, j)

        @pl.when(has1)
        def _():
            got(MATE1, j)

        @pl.when(has2)
        def _():
            got(MATE2, j)

        @pl.when(has_cross & has1)
        def _():
            got(CROSS1, j)

        @pl.when(has_cross & has2 & jnp.logical_not(along(j) & odd))
        def _():
            got(CROSS2, j)

        attend(j)

    def step(i, carry):
        for lead, stage in ((LEAD_OWN, stage_own), (LEAD_1, stage_1), (LEAD_2, stage_2), (0, stage_3)):
            j = i - LEAD_OWN + lead

            @pl.when((j >= 0) & (j < chunks))
            def _(j=j, stage=stage):
                stage(j)

        return carry

    lax.fori_loop(0, chunks + LEAD_OWN, step, 0)

    def finish(j, carry):
        flow = along(j)
        stay = jnp.logical_not(flow)
        sent(MATE0, j)
        for kind, there in (
            (CROSS0, has_cross),
            (SAME2, up),
            (SAME1, even | has2),
            (MATE1, has1),
            (MATE2, has2),
            (CROSS1, has_cross & ((stay & has1) | (flow & (even | has2)))),
            (CROSS2, has_cross & ((stay & has2) | (flow & up))),
        ):

            @pl.when(there)
            def _(kind=kind):
                sent(kind, j)

        return carry

    lax.fori_loop(0, chunks, finish, 0)


def on_device(ns, nt, query_states, key_states, value_states, history, neighbours):
    _, rows, width = query_states.shape
    chunks = width // CHUNK
    vmem = pl.BlockSpec(memory_space=pltpu.VMEM)
    smem = pl.BlockSpec(memory_space=pltpu.SMEM)
    heads = width // HEAD_DIM
    pairs = rows * rows * 9 * heads
    out = pl.pallas_call(
        functools.partial(kernel, ns, nt),
        out_shape=jax.ShapeDtypeStruct((rows, width), jnp.bfloat16),
        in_specs=[smem, smem, vmem, vmem, vmem],
        out_specs=vmem,
        scratch_shapes=[
            pltpu.VMEM((8, rows, width), jnp.bfloat16),
            pltpu.VMEM((8, rows, width), jnp.bfloat16),
            pltpu.SemaphoreType.DMA((2, 8, chunks)),
            pltpu.SemaphoreType.DMA((2, 8, chunks)),
        ],
        compiler_params=pltpu.CompilerParams(
            collective_id=0, has_side_effects=True, vmem_limit_bytes=48 * 1024 * 1024
        ),
        cost_estimate=pl.CostEstimate(
            flops=4 * pairs * HEAD_DIM,
            bytes_accessed=8 * rows * width,
            transcendentals=pairs,
        ),
    )(
        history,
        neighbours.reshape(2),
        query_states.reshape(rows, width),
        key_states.reshape(rows, width),
        value_states.reshape(rows, width),
    )
    return out.reshape(1, rows, width)


def solution(mesh):
    placed = (
        P("tm", "space", None),
        P("tm", "space", None),
        P("tm", "space", None),
        P("tm"),
        P("tm", "space", None),
    )
    return jax.shard_map(
        functools.partial(on_device, mesh.shape["tm"], mesh.shape["space"]),
        mesh=mesh,
        in_specs=placed,
        out_specs=P("tm", "space", None),
        check_vma=False,
    )
```

```python
import functools
import math

import jax
import jax.numpy as jnp
from jax import lax
from jax.experimental import pallas as pl
from jax.experimental.pallas import tpu as pltpu
from jax.sharding import PartitionSpec as P

HEAD_DIM = 128
CHUNK = 128
MATE0, CROSS0, SAME2, SAME1, MATE1, MATE2, CROSS1, CROSS2 = range(8)
BIG = 1e30
LEAD_OWN = 10
LEAD_1 = 6
LEAD_2 = 5
ALONG = 0.3


def kernel(
    ns, nt, hist_ref, side_ref, q_hbm, k_hbm, v_hbm, o_hbm,
    q_ref, k_ref, v_ref, o_ref, kbuf, vbuf, send_sem, recv_sem, in_sem, out_sem,
):
    rows, width = k_ref.shape
    chunks = width // CHUNK
    s = lax.axis_index("tm")
    t = lax.axis_index("space")
    odd = lax.rem(s, 2) == 1
    even = jnp.logical_not(odd)
    t_odd = lax.rem(t, 2) == 1
    mate = jnp.where(t_odd, t - 1, t + 1)
    cross = jnp.where(t_odd, t + 1, t - 1)
    pair = jnp.where(odd, s - 1, s + 1)
    has_cross = (cross >= 0) & (cross < nt)
    up = s + 2 < ns
    has1 = s >= 1
    has2 = s >= 2

    loads = [
        pltpu.make_async_copy(src, dst, in_sem.at[index])
        for index, (src, dst) in enumerate(((q_hbm, q_ref), (k_hbm, k_ref), (v_hbm, v_ref)))
    ]

    barrier = pltpu.get_barrier_semaphore()

    def greet(ss, tt):
        pl.semaphore_signal(
            barrier, inc=1, device_id=(ss, tt), device_id_type=pl.DeviceIdType.MESH
        )

    greet(s, mate)
    greet(pair, t)

    @pl.when(has_cross)
    def _():
        greet(s, cross)

    @pl.when(up)
    def _():
        greet(s + 2, t)

    @pl.when(has2)
    def _():
        greet(s - 2, t)

    for load in loads:
        load.start()

    for missing, slots in (
        (jnp.logical_not(has1), (SAME1, MATE1)),
        (jnp.logical_not(has2), (SAME2, MATE2)),
        (jnp.logical_not(has_cross), (CROSS0,)),
        (jnp.logical_not(has_cross & has1), (CROSS1,)),
        (jnp.logical_not(has_cross & has2), (CROSS2,)),
    ):

        @pl.when(missing)
        def _(slots=slots):
            for slot in slots:
                kbuf[slot] = jnp.zeros((rows, width), kbuf.dtype)
                vbuf[slot] = jnp.zeros((rows, width), vbuf.dtype)

    peers = 2
    for there in (has_cross, up, has2):
        peers = peers + jnp.where(there, 1, 0)
    pl.semaphore_wait(barrier, peers)

    def cols(j):
        return pl.ds(pl.multiple_of(j * CHUNK, CHUNK), CHUNK)

    def copies(kind, j, source, ss, tt):
        where = cols(j)
        out = []
        for index, (own, buf) in enumerate(((k_hbm, kbuf), (v_hbm, vbuf))):
            src = own.at[:, where] if source is None else buf.at[source, :, where]
            out.append(
                pltpu.make_async_remote_copy(
                    src_ref=src,
                    dst_ref=buf.at[kind, :, where],
                    send_sem=send_sem.at[index, kind, j],
                    recv_sem=recv_sem.at[index, kind, j],
                    device_id=(ss, tt),
                    device_id_type=pl.DeviceIdType.MESH,
                )
            )
        return out

    def send(kind, j, source, ss, tt):
        for copy in copies(kind, j, source, ss, tt):
            copy.start()

    def got(kind, j):
        for copy in copies(kind, j, None, s, mate):
            copy.wait_recv()

    def sent(kind, j):
        for copy in copies(kind, j, None, s, mate):
            copy.wait_send()

    def along(j):
        return j >= chunks - int(ALONG * chunks)

    def stage_own(j):
        @pl.when(up)
        def _():
            send(SAME2, j, None, s + 2, t)

        @pl.when(even)
        def _():
            send(SAME1, j, None, pair, t)

        send(MATE0, j, None, s, mate)

    def stage_1(j):
        @pl.when(has2)
        def _():
            got(SAME2, j)

            @pl.when(odd)
            def _():
                send(SAME1, j, SAME2, pair, t)

            @pl.when(has_cross & jnp.logical_not(along(j)))
            def _():
                send(CROSS2, j, SAME2, s, cross)

            send(MATE2, j, SAME2, s, mate)

        @pl.when(has_cross & along(j))
        def _():
            got(CROSS0, j)

            @pl.when(up)
            def _():
                send(CROSS2, j, CROSS0, s + 2, t)

            @pl.when(even)
            def _():
                send(CROSS1, j, CROSS0, pair, t)

    def stage_2(j):
        @pl.when(has1)
        def _():
            got(SAME1, j)

            @pl.when(has_cross & jnp.logical_not(along(j)))
            def _():
                send(CROSS1, j, SAME1, s, cross)

            send(MATE1, j, SAME1, s, mate)

        @pl.when(has_cross & along(j) & has2 & odd)
        def _():
            got(CROSS2, j)
            send(CROSS1, j, CROSS2, pair, t)

    history = hist_ref[0]
    left = (side_ref[0] == 1) & (t > 0)
    right = (side_ref[1] == 1) & (t < nt - 1)
    mate_ok = (t_odd & left) | (jnp.logical_not(t_odd) & right)
    cross_ok = (t_odd & right) | (jnp.logical_not(t_odd) & left)
    one_ok = (history >= 1) & has1
    two_ok = (history >= 2) & has2
    blocks = (
        (None, None),
        (MATE0, mate_ok),
        (CROSS0, cross_ok),
        (SAME1, one_ok),
        (MATE1, one_ok & mate_ok),
        (CROSS1, one_ok & cross_ok),
        (SAME2, two_ok),
        (MATE2, two_ok & mate_ok),
        (CROSS2, two_ok & cross_ok),
    )
    shifts = [
        None if ok is None else jnp.where(ok, jnp.float32(0.0), jnp.float32(BIG))
        for _, ok in blocks
    ]
    factor = math.log2(math.e) / HEAD_DIM**0.5

    def store(j):
        return pltpu.make_async_copy(o_ref.at[:, cols(j)], o_hbm.at[:, cols(j)], out_sem.at[j])

    def attend(j):
        for part in range(CHUNK // HEAD_DIM):
            where = pl.ds(pl.multiple_of(j * CHUNK + part * HEAD_DIM, HEAD_DIM), HEAD_DIM)
            q = q_ref[:, where]
            scores = []
            top = None
            for (slot, _), shift in zip(blocks, shifts):
                k = k_ref[:, where] if slot is None else kbuf[slot, :, where]
                score = lax.dot_general(
                    q, k, (((1,), (1,)), ((), ())), preferred_element_type=jnp.float32
                )
                scores.append(score)
                top = score if slot is None else jnp.maximum(top, score - shift)
            best = jnp.max(top, axis=1, keepdims=True) * factor
            total = None
            accum = None
            for (slot, _), shift, score in zip(blocks, shifts, scores):
                v = v_ref[:, where] if slot is None else vbuf[slot, :, where]
                floor = best if slot is None else best + shift
                weights = jnp.exp2(score * factor - floor)
                total = weights if slot is None else total + weights
                term = lax.dot_general(
                    weights.astype(jnp.bfloat16),
                    v,
                    (((1,), (0,)), ((), ())),
                    preferred_element_type=jnp.float32,
                )
                accum = term if slot is None else accum + term
            denom = jnp.sum(total, axis=1, keepdims=True)
            o_ref[:, where] = (accum / denom).astype(o_ref.dtype)
        store(j).start()

    def stage_3(j):
        got(MATE0, j)

        @pl.when(has_cross & jnp.logical_not(along(j)))
        def _():
            got(CROSS0, j)

        @pl.when(has1)
        def _():
            got(MATE1, j)

        @pl.when(has2)
        def _():
            got(MATE2, j)

        @pl.when(has_cross & has1)
        def _():
            got(CROSS1, j)

        @pl.when(has_cross & has2 & jnp.logical_not(along(j) & odd))
        def _():
            got(CROSS2, j)

        attend(j)

    def step(i, carry):
        @pl.when(has_cross & (i < chunks))
        def _():
            send(CROSS0, i, None, s, cross)

        for lead, stage in ((LEAD_OWN, stage_own), (LEAD_1, stage_1), (LEAD_2, stage_2), (0, stage_3)):
            j = i - LEAD_OWN + lead

            @pl.when((j >= 0) & (j < chunks))
            def _(j=j, stage=stage):
                stage(j)

        return carry

    for load in loads:
        load.wait()
    lax.fori_loop(0, chunks + LEAD_OWN, step, 0)

    def finish(j, carry):
        flow = along(j)
        stay = jnp.logical_not(flow)
        sent(MATE0, j)
        store(j).wait()
        for kind, there in (
            (CROSS0, has_cross),
            (SAME2, up),
            (SAME1, even | has2),
            (MATE1, has1),
            (MATE2, has2),
            (CROSS1, has_cross & ((stay & has1) | (flow & (even | has2)))),
            (CROSS2, has_cross & ((stay & has2) | (flow & up))),
        ):

            @pl.when(there)
            def _(kind=kind):
                sent(kind, j)

        return carry

    lax.fori_loop(0, chunks, finish, 0)


def on_device(ns, nt, query_states, key_states, value_states, history, neighbours):
    _, rows, width = query_states.shape
    chunks = width // CHUNK
    hbm = pl.BlockSpec(memory_space=pl.ANY)
    smem = pl.BlockSpec(memory_space=pltpu.SMEM)
    heads = width // HEAD_DIM
    pairs = rows * rows * 9 * heads
    out = pl.pallas_call(
        functools.partial(kernel, ns, nt),
        out_shape=jax.ShapeDtypeStruct((rows, width), jnp.bfloat16),
        in_specs=[smem, smem, hbm, hbm, hbm],
        out_specs=hbm,
        scratch_shapes=[
            pltpu.VMEM((rows, width), jnp.bfloat16),
            pltpu.VMEM((rows, width), jnp.bfloat16),
            pltpu.VMEM((rows, width), jnp.bfloat16),
            pltpu.VMEM((rows, width), jnp.bfloat16),
            pltpu.VMEM((8, rows, width), jnp.bfloat16),
            pltpu.VMEM((8, rows, width), jnp.bfloat16),
            pltpu.SemaphoreType.DMA((2, 8, chunks)),
            pltpu.SemaphoreType.DMA((2, 8, chunks)),
            pltpu.SemaphoreType.DMA((3,)),
            pltpu.SemaphoreType.DMA((chunks,)),
        ],
        compiler_params=pltpu.CompilerParams(
            collective_id=0, has_side_effects=True, vmem_limit_bytes=60 * 1024 * 1024
        ),
        cost_estimate=pl.CostEstimate(
            flops=4 * pairs * HEAD_DIM,
            bytes_accessed=8 * rows * width,
            transcendentals=pairs,
        ),
    )(
        history,
        neighbours.reshape(2),
        query_states.reshape(rows, width),
        key_states.reshape(rows, width),
        value_states.reshape(rows, width),
    )
    return out.reshape(1, rows, width)


def solution(mesh):
    placed = (
        P("tm", "space", None),
        P("tm", "space", None),
        P("tm", "space", None),
        P("tm"),
        P("tm", "space", None),
    )
    return jax.shard_map(
        functools.partial(on_device, mesh.shape["tm"], mesh.shape["space"]),
        mesh=mesh,
        in_specs=placed,
        out_specs=P("tm", "space", None),
        check_vma=False,
    )
```

```python
import functools
import math

import jax
import jax.numpy as jnp
from jax import lax
from jax.experimental import pallas as pl
from jax.experimental.pallas import tpu as pltpu
from jax.sharding import PartitionSpec as P

HEAD_DIM = 128
CHUNK = 128
MATE0, CROSS0, SAME2, SAME1, MATE1, MATE2, CROSS1, CROSS2 = range(8)
BIG = 1e30
LEAD_OWN = 10
LEAD_1 = 6
LEAD_2 = 5
ALONG = 0.3


def kernel(
    ns, nt, hist_ref, side_ref, q_hbm, k_hbm, v_hbm, o_hbm,
    q_ref, k_ref, v_ref, o_ref, kbuf, vbuf, send_sem, recv_sem, in_sem, out_sem,
):
    rows, width = k_ref.shape
    chunks = width // CHUNK
    s = lax.axis_index("tm")
    t = lax.axis_index("space")
    odd = lax.rem(s, 2) == 1
    even = jnp.logical_not(odd)
    t_odd = lax.rem(t, 2) == 1
    mate = jnp.where(t_odd, t - 1, t + 1)
    cross = jnp.where(t_odd, t + 1, t - 1)
    pair = jnp.where(odd, s - 1, s + 1)
    has_cross = (cross >= 0) & (cross < nt)
    up = s + 2 < ns
    has1 = s >= 1
    has2 = s >= 2

    loads = [
        pltpu.make_async_copy(src, dst, in_sem.at[index])
        for index, (src, dst) in enumerate(((q_hbm, q_ref), (k_hbm, k_ref), (v_hbm, v_ref)))
    ]

    barrier = pltpu.get_barrier_semaphore()

    def greet(ss, tt):
        pl.semaphore_signal(
            barrier, inc=1, device_id=(ss, tt), device_id_type=pl.DeviceIdType.MESH
        )

    greet(s, mate)
    greet(pair, t)

    @pl.when(has_cross)
    def _():
        greet(s, cross)

    @pl.when(up)
    def _():
        greet(s + 2, t)

    @pl.when(has2)
    def _():
        greet(s - 2, t)

    for load in loads:
        load.start()

    peers = 2
    for there in (has_cross, up, has2):
        peers = peers + jnp.where(there, 1, 0)
    pl.semaphore_wait(barrier, peers)

    def cols(j):
        return pl.ds(pl.multiple_of(j * CHUNK, CHUNK), CHUNK)

    def copies(kind, j, source, ss, tt):
        where = cols(j)
        out = []
        for index, (own, buf) in enumerate(((k_hbm, kbuf), (v_hbm, vbuf))):
            src = own.at[:, where] if source is None else buf.at[source, :, where]
            out.append(
                pltpu.make_async_remote_copy(
                    src_ref=src,
                    dst_ref=buf.at[kind, :, where],
                    send_sem=send_sem.at[index, kind, j],
                    recv_sem=recv_sem.at[index, kind, j],
                    device_id=(ss, tt),
                    device_id_type=pl.DeviceIdType.MESH,
                )
            )
        return out

    def send(kind, j, source, ss, tt):
        for copy in copies(kind, j, source, ss, tt):
            copy.start()

    def got(kind, j):
        for copy in copies(kind, j, None, s, mate):
            copy.wait_recv()

    def sent(kind, j):
        for copy in copies(kind, j, None, s, mate):
            copy.wait_send()

    def along(j):
        return j >= chunks - int(ALONG * chunks)

    def stage_own(j):
        @pl.when(up)
        def _():
            send(SAME2, j, None, s + 2, t)

        @pl.when(even)
        def _():
            send(SAME1, j, None, pair, t)

        send(MATE0, j, None, s, mate)

    def stage_1(j):
        @pl.when(has2)
        def _():
            got(SAME2, j)

            @pl.when(odd)
            def _():
                send(SAME1, j, SAME2, pair, t)

            @pl.when(has_cross & jnp.logical_not(along(j)))
            def _():
                send(CROSS2, j, SAME2, s, cross)

            send(MATE2, j, SAME2, s, mate)

        @pl.when(has_cross & along(j))
        def _():
            got(CROSS0, j)

            @pl.when(up)
            def _():
                send(CROSS2, j, CROSS0, s + 2, t)

            @pl.when(even)
            def _():
                send(CROSS1, j, CROSS0, pair, t)

    def stage_2(j):
        @pl.when(has1)
        def _():
            got(SAME1, j)

            @pl.when(has_cross & jnp.logical_not(along(j)))
            def _():
                send(CROSS1, j, SAME1, s, cross)

            send(MATE1, j, SAME1, s, mate)

        @pl.when(has_cross & along(j) & has2 & odd)
        def _():
            got(CROSS2, j)
            send(CROSS1, j, CROSS2, pair, t)

    history = hist_ref[0]
    left = (side_ref[0] == 1) & (t > 0)
    right = (side_ref[1] == 1) & (t < nt - 1)
    mate_ok = (t_odd & left) | (jnp.logical_not(t_odd) & right)
    cross_ok = (t_odd & right) | (jnp.logical_not(t_odd) & left)
    one_ok = (history >= 1) & has1
    two_ok = (history >= 2) & has2
    blocks = (
        (None, None),
        (MATE0, mate_ok),
        (CROSS0, cross_ok),
        (SAME1, one_ok),
        (MATE1, one_ok & mate_ok),
        (CROSS1, one_ok & cross_ok),
        (SAME2, two_ok),
        (MATE2, two_ok & mate_ok),
        (CROSS2, two_ok & cross_ok),
    )
    shifts = [
        None if ok is None else jnp.where(ok, jnp.float32(0.0), jnp.float32(BIG))
        for _, ok in blocks
    ]
    factor = math.log2(math.e) / HEAD_DIM**0.5

    def store(j):
        return pltpu.make_async_copy(o_ref.at[:, cols(j)], o_hbm.at[:, cols(j)], out_sem.at[j])

    def attend(j):
        for part in range(CHUNK // HEAD_DIM):
            where = pl.ds(pl.multiple_of(j * CHUNK + part * HEAD_DIM, HEAD_DIM), HEAD_DIM)
            q = q_ref[:, where]
            scores = []
            top = None
            for (slot, _), shift in zip(blocks, shifts):
                k = k_ref[:, where] if slot is None else kbuf[slot, :, where]
                score = lax.dot_general(
                    q, k, (((1,), (1,)), ((), ())), preferred_element_type=jnp.float32
                )
                scores.append(score)
                top = score if slot is None else jnp.maximum(top, score - shift)
            best = jnp.max(top, axis=1, keepdims=True) * factor
            total = None
            accum = None
            for (slot, _), shift, score in zip(blocks, shifts, scores):
                v = v_ref[:, where] if slot is None else vbuf[slot, :, where]
                floor = best if slot is None else best + shift
                weights = jnp.exp2(score * factor - floor)
                total = weights if slot is None else total + weights
                term = lax.dot_general(
                    weights.astype(jnp.bfloat16),
                    v,
                    (((1,), (0,)), ((), ())),
                    preferred_element_type=jnp.float32,
                )
                accum = term if slot is None else accum + term
            denom = jnp.sum(total, axis=1, keepdims=True)
            o_ref[:, where] = (accum / denom).astype(o_ref.dtype)
        store(j).start()

    def stage_3(j):
        got(MATE0, j)

        @pl.when(has_cross & jnp.logical_not(along(j)))
        def _():
            got(CROSS0, j)

        @pl.when(has1)
        def _():
            got(MATE1, j)

        @pl.when(has2)
        def _():
            got(MATE2, j)

        @pl.when(has_cross & has1)
        def _():
            got(CROSS1, j)

        @pl.when(has_cross & has2 & jnp.logical_not(along(j) & odd))
        def _():
            got(CROSS2, j)

        attend(j)

    def clear():
        for missing, slots in (
            (jnp.logical_not(has1), (SAME1, MATE1)),
            (jnp.logical_not(has2), (SAME2, MATE2)),
            (jnp.logical_not(has_cross), (CROSS0,)),
            (jnp.logical_not(has_cross & has1), (CROSS1,)),
            (jnp.logical_not(has_cross & has2), (CROSS2,)),
        ):

            @pl.when(missing)
            def _(slots=slots):
                for slot in slots:
                    kbuf[slot] = jnp.zeros((rows, width), kbuf.dtype)
                    vbuf[slot] = jnp.zeros((rows, width), vbuf.dtype)

    def step(i, carry):
        pl.when(i == 3)(clear)

        @pl.when(has_cross & (i < chunks))
        def _():
            send(CROSS0, i, None, s, cross)

        for lead, stage in ((LEAD_OWN, stage_own), (LEAD_1, stage_1), (LEAD_2, stage_2), (0, stage_3)):
            j = i - LEAD_OWN + lead

            @pl.when((j >= 0) & (j < chunks))
            def _(j=j, stage=stage):
                stage(j)

        return carry

    for load in loads:
        load.wait()
    lax.fori_loop(0, chunks + LEAD_OWN, step, 0)

    def finish(j, carry):
        flow = along(j)
        stay = jnp.logical_not(flow)
        sent(MATE0, j)
        store(j).wait()
        for kind, there in (
            (CROSS0, has_cross),
            (SAME2, up),
            (SAME1, even | has2),
            (MATE1, has1),
            (MATE2, has2),
            (CROSS1, has_cross & ((stay & has1) | (flow & (even | has2)))),
            (CROSS2, has_cross & ((stay & has2) | (flow & up))),
        ):

            @pl.when(there)
            def _(kind=kind):
                sent(kind, j)

        return carry

    lax.fori_loop(0, chunks, finish, 0)


def on_device(ns, nt, query_states, key_states, value_states, history, neighbours):
    _, rows, width = query_states.shape
    chunks = width // CHUNK
    hbm = pl.BlockSpec(memory_space=pl.ANY)
    smem = pl.BlockSpec(memory_space=pltpu.SMEM)
    heads = width // HEAD_DIM
    pairs = rows * rows * 9 * heads
    out = pl.pallas_call(
        functools.partial(kernel, ns, nt),
        out_shape=jax.ShapeDtypeStruct((rows, width), jnp.bfloat16),
        in_specs=[smem, smem, hbm, hbm, hbm],
        out_specs=hbm,
        scratch_shapes=[
            pltpu.VMEM((rows, width), jnp.bfloat16),
            pltpu.VMEM((rows, width), jnp.bfloat16),
            pltpu.VMEM((rows, width), jnp.bfloat16),
            pltpu.VMEM((rows, width), jnp.bfloat16),
            pltpu.VMEM((8, rows, width), jnp.bfloat16),
            pltpu.VMEM((8, rows, width), jnp.bfloat16),
            pltpu.SemaphoreType.DMA((2, 8, chunks)),
            pltpu.SemaphoreType.DMA((2, 8, chunks)),
            pltpu.SemaphoreType.DMA((3,)),
            pltpu.SemaphoreType.DMA((chunks,)),
        ],
        compiler_params=pltpu.CompilerParams(
            collective_id=0, has_side_effects=True, vmem_limit_bytes=60 * 1024 * 1024
        ),
        cost_estimate=pl.CostEstimate(
            flops=4 * pairs * HEAD_DIM,
            bytes_accessed=8 * rows * width,
            transcendentals=pairs,
        ),
    )(
        history,
        neighbours.reshape(2),
        query_states.reshape(rows, width),
        key_states.reshape(rows, width),
        value_states.reshape(rows, width),
    )
    return out.reshape(1, rows, width)


def solution(mesh):
    placed = (
        P("tm", "space", None),
        P("tm", "space", None),
        P("tm", "space", None),
        P("tm"),
        P("tm", "space", None),
    )
    return jax.shard_map(
        functools.partial(on_device, mesh.shape["tm"], mesh.shape["space"]),
        mesh=mesh,
        in_specs=placed,
        out_specs=P("tm", "space", None),
        check_vma=False,
    )
```
